512 devices in a mesh: dp: 8 (over z), seq: 16 (over y, core), mp: 4 (over x).
Axes of the slice: x: 4, y: 8, z: 8, core: 2. Of those that a mesh axis runs over, the one named last changes fastest.
Arguments:
- tokens: bfloat16 [65536, 4096], P(('dp', 'seq'), 'mp'), parts along dimension 0, may hold values from -30 to 30
- heavy_index: int32 [8192], P(('dp', 'seq')), parts along dimension 0, may hold values from -1 to 8191, as said below
- norm_gain: float32 [4096], P('mp'), may hold values from 0.1 to 1.9
- router: bfloat16 [4096], P('mp'), may hold values from -0.09375 to 0.09375
- w_up: bfloat16 [4096, 8192], P('mp', 'seq'), may hold values from -0.09375 to 0.09375
- w_down: bfloat16 [8192, 4096], P('seq', 'mp'), may hold values from -0.0625 to 0.0625
Outputs:
- mixed: bfloat16 [65536, 4096], P(('dp', 'seq'), 'mp'), parts along dimension 0
The draws below stay inside these ranges and needn't reach their ends.
There are 8 independent parts, one for each index of `dp`. The reference program is written for one: setup_inputs(seed, part) draws one part's arguments, and reference() takes and returns one part's arrays. A program takes and returns all parts, laid end to end along the dimension named above; an argument that names none is the same for every part. Nothing has to cross between parts.
Inputs may be any that keep to these rules, and one draw needn't show every extreme that they name: `heavy_index`: the 64 slots of each index of seq hold, in rising order, the positions of that index's own routed tokens, then -1. Every index has 0 to 64 routed tokens, some index exactly 64, and all together exactly 512.
All inputs are finite; a program needn't handle non-finite values.
Results may differ from the reference program's by a relative error of at most 0.0035.
Values may be sent and summed in bfloat16 or wider, within the bound.
No kernel may reach another device: no remote copies, remote signals or barrier semaphores. Data moves between devices by JAX's collectives and lax.ppermute only.
A program may use at most 64 MiB of HBM per device.

```python
import math
import jax
import jax.numpy as jnp
from jax import lax

D = 4096
FF = 8192
TOK_DEV = 512
SEQ_LEN = 8192
CAP = 64


def draw_tokens(key, part):
    key = jax.random.fold_in(key, 11)
    base_key, row_key, col_key = jax.random.split(key, 3)
    rising = 1.0 + 2.0 * jnp.arange(D, dtype=jnp.float32) / D
    col_scale = jnp.exp(jax.random.uniform(col_key, (D,), jnp.float32, math.log(0.5), math.log(2.0))) * rising / 2.1
    row_scale = jnp.exp(jax.random.uniform(row_key, (SEQ_LEN, 1), jnp.float32, math.log(0.5), math.log(2.0)))
    noise = jnp.clip(jax.random.normal(base_key, (SEQ_LEN, D), jnp.float32), -4.0, 4.0)
    values = noise * col_scale * row_scale
    return values.astype(jnp.bfloat16)


def draw_heavy_index(key, part):
    key = jax.random.fold_in(key, 7)
    pair_key, delta_key, shard_key = jax.random.split(key, 3)
    shards = SEQ_LEN // TOK_DEV
    average = TOK_DEV // 16
    capacity = CAP
    pairing = jax.random.permutation(pair_key, shards)
    deltas = jax.random.randint(delta_key, (shards // 2,), -average, average + 1)
    deltas = deltas.at[0].set(average)
    rank_counts = jnp.stack([average + deltas, average - deltas], axis=1).reshape(-1)
    all_counts = jnp.zeros((shards,), jnp.int32).at[pairing].set(rank_counts.astype(jnp.int32))
    shard_keys = jax.random.split(shard_key, shards)
    shuffled = jax.vmap(lambda one_key: jax.random.permutation(one_key, TOK_DEV))(shard_keys)
    chosen = shuffled < all_counts[:, None]
    token_iota = jnp.arange(TOK_DEV, dtype=jnp.int32)[None, :]
    ranked = jnp.argsort(jnp.where(chosen, 0, 1) * TOK_DEV + token_iota, axis=1)
    positions = ranked[:, :capacity].astype(jnp.int32)
    slot_iota = jnp.arange(capacity, dtype=jnp.int32)[None, :]
    shard_start = (jnp.arange(shards, dtype=jnp.int32) * TOK_DEV)[:, None]
    entries = jnp.where(slot_iota < all_counts[:, None], positions + shard_start, -1)
    return entries.reshape(-1).astype(jnp.int32)


def shard_levels(stream_key, dims, cuts, least, top_value):
    def one(axis_at, shards_of):
        steps = jax.random.uniform(jax.random.fold_in(jax.random.fold_in(stream_key, 6), axis_at), (shards_of,), jnp.float32, least / len(cuts), top_value / len(cuts))
        return jnp.repeat(jnp.exp(steps), dims[axis_at] // shards_of).reshape((-1,) + (1,) * (len(dims) - axis_at - 1))

    loudness = one(*cuts[0])
    for cut in cuts[1:]:
        loudness = loudness * one(*cut)
    return loudness


def normal_values(own_key, shape, deviation, bound, cuts=(), kind=jnp.bfloat16):
    array = deviation * jax.random.normal(own_key, shape, jnp.float32)
    if cuts:
        array = array * shard_levels(own_key, shape, cuts, -0.22, 0.18)
    return jnp.clip(array, -bound, bound).astype(kind)


def setup_inputs(seed: int = 0, part: int = 0) -> dict:
    streams_of = jax.random.split(jax.random.key(seed), 7)
    part_keys = jax.random.split(jax.random.fold_in(streams_of[6], part), 7)
    return {
        "tokens": draw_tokens(jax.random.fold_in(jax.random.fold_in(streams_of[6], part), 71), part),
        "heavy_index": draw_heavy_index(jax.random.fold_in(jax.random.fold_in(streams_of[6], part), 71), part),
        "norm_gain": jnp.clip(1.0 + 0.18 * jax.random.normal(streams_of[2], (D,), jnp.float32), 0.1, 1.9),
        "router": normal_values(streams_of[3], (D,), D ** -0.5, 0.09375, ((0, 4),)),
        "w_up": normal_values(streams_of[4], (D, FF), D ** -0.5, 0.09375, ((0, 4), (1, 16))),
        "w_down": normal_values(streams_of[5], (FF, D), FF ** -0.5, 0.0625, ((0, 16), (1, 4))),
    }


def reference(tokens, heavy_index, norm_gain, router, w_up, w_down):
    is_valid = heavy_index >= 0
    safe_index = jnp.where(is_valid, heavy_index, 0).astype(jnp.int32)
    selected = tokens[safe_index].astype(jnp.float32) * is_valid[:, None].astype(jnp.float32)
    square_sums = lax.optimization_barrier(jnp.sum(selected * selected, axis=1))
    inverse = lax.rsqrt(square_sums / D + 1e-06)
    logits = lax.optimization_barrier(jnp.sum(selected * (norm_gain * router.astype(jnp.float32)), axis=1)) * inverse
    scores = jax.nn.sigmoid(logits)
    normed = (selected * inverse[:, None] * norm_gain).astype(jnp.bfloat16)
    upward = jnp.dot(normed, w_up, preferred_element_type=jnp.float32)
    hidden = jax.nn.gelu(upward, approximate=True).astype(jnp.bfloat16)
    heavy_out = jnp.dot(hidden, w_down, preferred_element_type=jnp.float32)
    addition = scores[:, None] * heavy_out * is_valid[:, None].astype(jnp.float32)
    mixed = tokens.astype(jnp.float32).at[safe_index].add(addition)
    return mixed.astype(jnp.bfloat16)
```

```python
import jax
import jax.numpy as jnp
from jax import lax
from jax.sharding import Mesh, PartitionSpec as P

D = 4096
BF = jnp.bfloat16
F32 = jnp.float32


def halves(value):
    high = value.astype(BF)
    return high, (value - high.astype(F32)).astype(BF)


def per_device(tokens, heavy_index, norm_gain, router, w_up, w_down):
    tok_rows, width = tokens.shape
    slots = heavy_index.shape[0]
    hidden_width = w_up.shape[1]
    chips = lax.axis_size("y")
    parts = lax.axis_size("mp")
    cores = [(0, 1), (1, 0)]
    seq_rank = lax.axis_index("y") * 2 + lax.axis_index("core")
    local_index = heavy_index - seq_rank * tok_rows
    hits = local_index[:, None] == jnp.arange(tok_rows, dtype=jnp.int32)[None, :]
    picker = hits.astype(BF)
    selected = jnp.dot(picker, tokens, preferred_element_type=F32).astype(BF)

    spread = jnp.broadcast_to(selected[None], (chips, slots, width))
    mine = lax.all_to_all(spread, "y", 0, 0, tiled=True).reshape(chips * slots, width)
    other = lax.ppermute(mine, "core", cores)
    rows = jnp.concatenate([mine, other])
    total = rows.shape[0]
    chunk = total // parts

    raw = rows.astype(F32)
    square_part = jnp.sum(raw * raw, axis=1)
    router_part = jnp.sum(raw * (norm_gain * router.astype(F32)), axis=1)
    up_part = jnp.dot((raw * norm_gain).astype(BF), w_up, preferred_element_type=F32).astype(BF)
    sums = jnp.stack([square_part.reshape(parts, chunk), router_part.reshape(parts, chunk)], axis=1)
    sums = jnp.stack(halves(sums), axis=2).reshape(parts, -1, hidden_width)
    sums = jnp.pad(sums, ((0, 0), (0, 16 - sums.shape[1]), (0, 0)))
    packed = jnp.concatenate([up_part.reshape(parts, chunk, hidden_width), sums], axis=1)
    packed = lax.all_to_all(packed, "mp", 0, 0, tiled=True).astype(F32)
    summed = jnp.sum(packed, axis=0)
    sums = summed[chunk:].reshape(-1)[: 4 * chunk].reshape(2, 2, chunk).sum(axis=1)
    inverse = lax.rsqrt(sums[0] / D + 1e-06)
    scores = jax.nn.sigmoid(sums[1] * inverse)
    hidden = jax.nn.gelu(summed[:chunk] * inverse[:, None], approximate=True) * scores[:, None]
    hidden = jnp.broadcast_to(hidden.astype(BF)[None], (parts, chunk, hidden_width))
    hidden = lax.all_to_all(hidden, "mp", 0, 0, tiled=True).reshape(total, hidden_width)

    down = jnp.dot(hidden, w_down, preferred_element_type=F32)
    half = total // 2
    away = lax.ppermute(down[half:].astype(BF), "core", cores)
    chip_sum = (down[:half] + away.astype(F32)).astype(BF).reshape(chips, slots, width)
    addition = jnp.sum(lax.all_to_all(chip_sum, "y", 0, 0, tiled=True).astype(F32), axis=0)
    placed = jnp.dot(picker.T.astype(F32), addition, precision=lax.Precision.HIGHEST)
    return (tokens.astype(F32) + placed).astype(BF)


def solution(mesh):
    dp, seq, mp = mesh.devices.shape
    fine = Mesh(mesh.devices.reshape(dp, seq // 2, 2, mp), ("dp", "y", "core", "mp"))
    seq = ("y", "core")
    rows = ("dp",) + seq
    placed = (P(rows, "mp"), P(rows), P("mp"), P("mp"), P("mp", seq), P(seq, "mp"))
    return jax.shard_map(
        per_device, mesh=fine, in_specs=placed, out_specs=P(rows, "mp"), check_vma=False
    )
```

```python
import jax
import jax.numpy as jnp
from jax import lax
from jax.sharding import Mesh, PartitionSpec as P

D = 4096
ROUTED = 512
EMPTY = 31.5
LIMIT = 30.5
SCALE = 2048.0
BF = jnp.bfloat16
F16 = jnp.float16
F32 = jnp.float32
I32 = jnp.int32


def halves(value):
    high = value.astype(BF)
    return high, (value - high.astype(F32)).astype(BF)


def per_device(tokens, heavy_index, norm_gain, router, w_up, w_down):
    tok_rows, width = tokens.shape
    slots = heavy_index.shape[0]
    hidden_width = w_up.shape[1]
    chips = lax.axis_size("y")
    parts = lax.axis_size("mp")
    core = lax.axis_index("core")
    owners = 2 * chips
    used_rows = ROUTED
    chunk = used_rows // parts
    seq_rank = lax.axis_index("y") * 2 + core
    local_index = heavy_index - seq_rank * tok_rows
    token_iota = jnp.arange(tok_rows, dtype=I32)
    picker = (local_index[:, None] == token_iota[None, :]).astype(BF)
    selected = jnp.dot(picker, tokens, preferred_element_type=F32)
    selected = jnp.where(heavy_index[:, None] >= 0, selected, EMPTY)

    rows = lax.all_gather((selected * SCALE).astype(F16), ("y", "core"), tiled=True)
    rows = (rows.astype(F32) * (1.0 / SCALE)).astype(BF)

    used = (rows[:, 0].reshape(owners, slots) < LIMIT).astype(I32)
    counts = jnp.sum(used, axis=1)
    earlier = jnp.arange(owners)[None, :] < jnp.arange(owners)[:, None]
    first = jnp.sum(jnp.where(earlier, counts[None, :], 0), axis=1)
    slot_iota = jnp.arange(slots, dtype=I32)
    place = jnp.where(slot_iota[None] < counts[:, None], first[:, None] + slot_iota[None], -1)
    row_iota = jnp.arange(used_rows, dtype=I32)
    compactor = (row_iota[:, None] == place.reshape(owners * slots)[None, :]).astype(BF)
    raw = jnp.dot(compactor, rows, preferred_element_type=F32)

    square_part = jnp.sum(raw * raw, axis=1).reshape(parts, 1, chunk)
    router_part = jnp.sum(raw * (norm_gain * router.astype(F32)), axis=1).reshape(parts, 1, chunk)
    up_part = jnp.dot((raw * norm_gain).astype(BF), w_up, preferred_element_type=F32).astype(BF)
    sums = jnp.concatenate([square_part, router_part], axis=1)
    sums = jnp.pad(sums, ((0, 0), (0, 14), (0, hidden_width // 2 - chunk)))
    packed = jnp.concatenate(
        [up_part.reshape(parts, chunk, hidden_width), jnp.concatenate(halves(sums), axis=2)], axis=1
    )
    summed = jnp.sum(lax.all_to_all(packed, "mp", 0, 0, tiled=True).astype(F32), axis=0)
    sums = summed[chunk : chunk + 2].reshape(2, 2, -1).sum(axis=1)[:, :chunk]
    inverse = lax.rsqrt(sums[0] / D + 1e-06)
    scores = jax.nn.sigmoid(sums[1] * inverse)
    hidden = jax.nn.gelu(summed[:chunk] * inverse[:, None], approximate=True) * scores[:, None]
    hidden = jnp.broadcast_to(hidden.astype(BF)[None], (parts, chunk, hidden_width))
    hidden = lax.all_to_all(hidden, "mp", 0, 0, tiled=True).reshape(used_rows, hidden_width)

    pairs = place.reshape(chips, 2, slots)
    swapped = jnp.where(core == 0, pairs, pairs[:, ::-1])
    ordered = swapped.transpose(1, 0, 2).reshape(owners * slots)
    expander = (ordered[:, None] == row_iota[None, :]).astype(BF)
    hidden = jnp.dot(expander, hidden, preferred_element_type=F32).astype(BF)
    down = jnp.dot(hidden, w_down, preferred_element_type=F32)
    half = chips * slots
    away = lax.ppermute(down[half:].astype(BF), "core", [(0, 1), (1, 0)])
    chip_sum = (down[:half] + away.astype(F32)).astype(BF).reshape(chips, slots, width)
    addition = jnp.sum(lax.all_to_all(chip_sum, "y", 0, 0, tiled=True).astype(F32), axis=0)
    placed = jnp.dot(picker.T.astype(F32), addition, precision=lax.Precision.HIGHEST)
    return (tokens.astype(F32) + placed).astype(BF)


def solution(mesh):
    dp, seq, mp = mesh.devices.shape
    fine = Mesh(mesh.devices.reshape(dp, seq // 2, 2, mp), ("dp", "y", "core", "mp"))
    seq = ("y", "core")
    rows = ("dp",) + seq
    placed = (P(rows, "mp"), P(rows), P("mp"), P("mp"), P("mp", seq), P(seq, "mp"))
    return jax.shard_map(
        per_device, mesh=fine, in_specs=placed, out_specs=P(rows, "mp"), check_vma=False
    )
```

```python
import jax
import jax.numpy as jnp
from jax import lax
from jax.sharding import Mesh, PartitionSpec as P

D = 4096
ROUTED = 512
EMPTY = 31.5
LIMIT = 30.5
SCALE = 2048.0
BF = jnp.bfloat16
F16 = jnp.float16
F32 = jnp.float32
I32 = jnp.int32


def halves(value):
    high = value.astype(BF)
    return high, (value - high.astype(F32)).astype(BF)


def per_device(tokens, heavy_index, norm_gain, router, w_up, w_down):
    tok_rows, width = tokens.shape
    slots = heavy_index.shape[0]
    hidden_width = w_up.shape[1]
    chips = lax.axis_size("y")
    parts = lax.axis_size("mp")
    core = lax.axis_index("core")
    owners = 2 * chips
    used_rows = ROUTED
    chunk = used_rows // parts
    seq_rank = lax.axis_index("y") * 2 + core
    local_index = heavy_index - seq_rank * tok_rows
    token_iota = jnp.arange(tok_rows, dtype=I32)
    picker = (local_index[:, None] == token_iota[None, :]).astype(BF)
    selected = jnp.dot(picker, tokens, preferred_element_type=F32)
    selected = jnp.where(local_index[:, None] >= 0, selected, EMPTY)

    rows = lax.all_gather((selected * SCALE).astype(F16), ("y", "core"), tiled=True)
    marks = rows[:, :1].astype(F32).reshape(owners, slots)
    counts = jnp.sum((marks < LIMIT * SCALE).astype(I32), axis=1)
    rows = (rows.astype(F32) * (1.0 / SCALE)).astype(BF)
    earlier = jnp.arange(owners)[None, :] < jnp.arange(owners)[:, None]
    first = jnp.sum(jnp.where(earlier, counts[None, :], 0), axis=1)
    slot_iota = jnp.arange(slots, dtype=I32)
    place = jnp.where(slot_iota[None] < counts[:, None], first[:, None] + slot_iota[None], -1)
    row_iota = jnp.arange(used_rows, dtype=I32)
    compactor = (row_iota[:, None] == place.reshape(owners * slots)[None, :]).astype(BF)
    raw = jnp.dot(compactor, rows, preferred_element_type=F32)

    square_part = jnp.sum(raw * raw, axis=1).reshape(parts, 1, chunk)
    router_part = jnp.sum(raw * (norm_gain * router.astype(F32)), axis=1).reshape(parts, 1, chunk)
    up_part = jnp.dot((raw * norm_gain).astype(BF), w_up, preferred_element_type=F32).astype(BF)
    sums = jnp.concatenate([square_part, router_part], axis=1)
    sums = jnp.pad(sums, ((0, 0), (0, 14), (0, hidden_width // 2 - chunk)))
    packed = jnp.concatenate(
        [up_part.reshape(parts, chunk, hidden_width), jnp.concatenate(halves(sums), axis=2)], axis=1
    )
    pairs = place.reshape(chips, 2, slots)
    own_place = jnp.where(core == 0, pairs[:, 0], pairs[:, 1]).reshape(chips * slots)
    other_place = jnp.where(core == 0, pairs[:, 1], pairs[:, 0]).reshape(chips * slots)
    packed, own_place, other_place = lax.optimization_barrier((packed, own_place, other_place))
    summed = jnp.sum(lax.all_to_all(packed, "mp", 0, 0, tiled=True).astype(F32), axis=0)
    sums = summed[chunk : chunk + 2].reshape(2, 2, -1).sum(axis=1)[:, :chunk]
    inverse = lax.rsqrt(sums[0] / D + 1e-06)
    scores = jax.nn.sigmoid(sums[1] * inverse)
    hidden = jax.nn.gelu(summed[:chunk] * inverse[:, None], approximate=True) * scores[:, None]
    hidden = jnp.broadcast_to(hidden.astype(BF)[None], (parts, chunk, hidden_width))
    hidden = lax.all_to_all(hidden, "mp", 0, 0, tiled=True).reshape(used_rows, hidden_width)

    def down(places):
        expander = (places[:, None] == row_iota[None, :]).astype(BF)
        wanted = jnp.dot(expander, hidden, preferred_element_type=F32).astype(BF)
        return jnp.dot(wanted, w_down, preferred_element_type=F32)

    away = lax.ppermute(down(other_place).astype(BF), "core", [(0, 1), (1, 0)])
    chip_sum = (down(own_place) + away.astype(F32)).astype(BF).reshape(chips, slots, width)
    targets = jnp.broadcast_to(local_index[None], (chips, slots)).reshape(chips * slots)
    chip_sum, targets = lax.optimization_barrier((chip_sum, targets))
    terms = lax.all_to_all(chip_sum, "y", 0, 0, tiled=True).reshape(chips * slots, width)
    placer = (targets[:, None] == token_iota[None, :]).astype(BF)
    placed = lax.dot_general(
        placer, terms, (((0,), (0,)), ((), ())), preferred_element_type=F32
    )
    return (tokens.astype(F32) + placed).astype(BF)


def solution(mesh):
    dp, seq, mp = mesh.devices.shape
    fine = Mesh(mesh.devices.reshape(dp, seq // 2, 2, mp), ("dp", "y", "core", "mp"))
    seq = ("y", "core")
    rows = ("dp",) + seq
    placed = (P(rows, "mp"), P(rows), P("mp"), P("mp"), P("mp", seq), P(seq, "mp"))
    return jax.shard_map(
        per_device, mesh=fine, in_specs=placed, out_specs=P(rows, "mp"), check_vma=False
    )
```

```python
import jax
import jax.numpy as jnp
from jax import lax
from jax.sharding import Mesh, PartitionSpec as P

D = 4096
ROUTED = 512
EMPTY = 31.5
LIMIT = 30.5
SCALE = 2048.0
BF = jnp.bfloat16
F16 = jnp.float16
F32 = jnp.float32
I32 = jnp.int32
PAIR = [(0, 1), (1, 0)]


def halves(value):
    high = value.astype(BF)
    return high, (value - high.astype(F32)).astype(BF)


def per_device(tokens, heavy_index, norm_gain, router, w_up, w_down):
    tok_rows, width = tokens.shape
    slots = heavy_index.shape[0]
    hidden_width = w_up.shape[1]
    chips = lax.axis_size("yh") * 2
    parts = lax.axis_size("mp")
    core = lax.axis_index("core")
    side = lax.axis_index("yl")
    owners = 2 * chips
    share = slots // 2
    piece = -(-(ROUTED + owners) // (2 * parts * 8)) * 8
    room = parts * piece
    chunk = 2 * piece
    seq_rank = (lax.axis_index("yh") * 2 + side) * 2 + core
    local_index = heavy_index - seq_rank * tok_rows
    token_iota = jnp.arange(tok_rows, dtype=I32)
    picker = (local_index[:, None] == token_iota[None, :]).astype(BF)
    selected = jnp.dot(picker, tokens, preferred_element_type=F32)
    selected = jnp.where(local_index[:, None] >= 0, selected, EMPTY)

    rows = lax.all_gather((selected * SCALE).astype(F16), ("yh", "yl", "core"), tiled=True)
    rows, w_here = lax.optimization_barrier((rows, w_down))
    early = hidden_width * 3 // 4
    w_early = lax.ppermute(w_here[:early], "yl", PAIR)
    marks = rows[:, :1].astype(F32).reshape(owners, slots)
    counts = jnp.sum((marks < LIMIT * SCALE).astype(I32), axis=1)
    rows = (rows.astype(F32) * (1.0 / SCALE)).astype(BF)

    parity = jnp.arange(2, dtype=I32)
    number = (counts[:, None] + 1 - parity[None, :]) // 2
    earlier = jnp.arange(owners)[None, :] < jnp.arange(owners)[:, None]
    first = jnp.sum(jnp.where(earlier[:, :, None], number[None], 0), axis=1)
    share_iota = jnp.arange(share, dtype=I32)
    in_use = share_iota[None, :, None] < number[:, None, :]
    place = jnp.where(in_use, first[:, None, :] + share_iota[None, :, None], -1)
    spot = place // piece * chunk + parity[None, None, :] * piece + place % piece
    spot = jnp.where(in_use, spot, -1).reshape(owners * slots)
    row_iota = jnp.arange(parts * chunk, dtype=I32)
    compactor = (row_iota[:, None] == spot[None, :]).astype(BF)
    raw = jnp.dot(compactor, rows, preferred_element_type=BF)
    raw = raw.astype(F32)

    square_part = jnp.sum(raw * raw, axis=1).reshape(parts, 1, chunk)
    router_part = jnp.sum(raw * (norm_gain * router.astype(F32)), axis=1).reshape(parts, 1, chunk)
    up_part = jnp.dot((raw * norm_gain).astype(BF), w_up, preferred_element_type=F32).astype(BF)
    sums = jnp.concatenate([square_part, router_part], axis=1)
    sums = jnp.pad(sums, ((0, 0), (0, 14), (0, hidden_width // 2 - chunk)))
    packed = jnp.concatenate(
        [up_part.reshape(parts, chunk, hidden_width), jnp.concatenate(halves(sums), axis=2)], axis=1
    )
    mine = jnp.where(side == 0, place[:, :, 0], place[:, :, 1]).reshape(chips, 2, share)
    ordered = jnp.where(core == 0, mine, mine[:, ::-1]).transpose(1, 0, 2).reshape(owners * share)
    packed, ordered = lax.optimization_barrier((packed, ordered))
    packed = lax.all_to_all(packed, "mp", 0, 0, tiled=True)
    packed, w_early, w_rest = lax.optimization_barrier((packed, w_early, w_here[early:]))
    w_late = lax.ppermute(w_rest, "yl", PAIR)
    summed = jnp.sum(packed.astype(F32), axis=0)
    sums = summed[chunk : chunk + 2].reshape(2, 2, -1).sum(axis=1)[:, :chunk]
    inverse = lax.rsqrt(sums[0] / D + 1e-06)
    scores = jax.nn.sigmoid(sums[1] * inverse)
    hidden = jax.nn.gelu(summed[:chunk] * inverse[:, None], approximate=True) * scores[:, None]
    hidden = hidden.astype(BF).reshape(2, 1, piece, hidden_width)
    hidden = jnp.broadcast_to(hidden, (2, parts, piece, hidden_width))
    hidden = lax.all_to_all(
        hidden.reshape(2 * parts, piece, hidden_width), ("yl", "mp"), 0, 0, tiled=True
    ).reshape(2, room, hidden_width)
    here = jnp.where(side == 0, hidden[0], hidden[1])
    near = jnp.where(side == 0, hidden[1], hidden[0])

    expander = (ordered[:, None] == jnp.arange(room, dtype=I32)[None, :]).astype(BF)
    wanted = jnp.dot(
        expander, jnp.concatenate([here, near], axis=1), preferred_element_type=F32
    ).astype(BF)
    wanted = lax.optimization_barrier(wanted)
    half = chips * share

    def down(some):
        total, at = 0.0, 0
        for w in (w_down, w_early, w_late):
            upto = at + w.shape[0]
            total += jnp.dot(some[:, at:upto], w, preferred_element_type=F32)
            at = upto
        return total

    away = lax.ppermute(down(wanted[half:]).astype(BF), "core", PAIR)
    chip_sum = (down(wanted[:half]) + away.astype(F32)).astype(BF).reshape(chips, share, width)
    targets = jnp.broadcast_to(local_index.reshape(share, 2).T[None], (chips // 2, 2, share))
    chip_sum, targets = lax.optimization_barrier((chip_sum, targets.reshape(chips * share)))
    terms = lax.all_to_all(chip_sum, ("yh", "yl"), 0, 0, tiled=True).reshape(chips * share, width)
    placer = (targets[:, None] == token_iota[None, :]).astype(BF)
    placed = lax.dot_general(
        placer, terms, (((0,), (0,)), ((), ())), preferred_element_type=F32
    )
    return (tokens.astype(F32) + placed).astype(BF)


def solution(mesh):
    dp, seq, mp = mesh.devices.shape
    names = ("dp", "yh", "yl", "core", "mp")
    fine = Mesh(mesh.devices.reshape(dp, seq // 4, 2, 2, mp), names)
    seq = names[1:4]
    rows = names[:4]
    placed = (P(rows, "mp"), P(rows), P("mp"), P("mp"), P("mp", seq), P(seq, "mp"))
    return jax.shard_map(
        per_device, mesh=fine, in_specs=placed, out_specs=P(rows, "mp"), check_vma=False
    )
```

```python
import functools

import jax
import jax.numpy as jnp
from jax import lax
from jax.experimental import pallas as pl
from jax.experimental.pallas import tpu as pltpu
from jax.sharding import Mesh, PartitionSpec as P

D = 4096
ROUTED = 512
EMPTY = 31.5
LIMIT = 30.5
SCALE = 2048.0
BF = jnp.bfloat16
F16 = jnp.float16
F32 = jnp.float32
I32 = jnp.int32


def iota(shape, axis):
    return lax.broadcasted_iota(I32, shape, axis)


def up_kernel(slots, core_ref, rows_ref, gain_ref, route_ref, w_ref, out_ref, place_ref):
    count = rows_ref.shape[0]
    parts, chunk = out_ref.shape[:2]
    total = parts * chunk
    hidden_width = w_ref.shape[1]
    core = core_ref[0]
    pick = (iota((8, 128), 1) == 0).astype(BF)
    marks = lax.dot_general(
        pick, rows_ref[:, :128], (((1,), (1,)), ((), ())), preferred_element_type=F32
    )
    used = (marks < LIMIT).astype(F32).astype(BF)
    owner = (iota((count, 128), 0) // slots == iota((count, 128), 1)).astype(BF)
    numbers = jnp.dot(used, owner, preferred_element_type=F32).astype(BF)

    def places(owner_of, length):
        lanes = iota((128, length), 0)
        before = (lanes < owner_of((128, length))).astype(BF)
        same = (lanes == owner_of((128, length))).astype(BF)
        first = jnp.dot(numbers, before, preferred_element_type=F32).astype(I32)
        number = jnp.dot(numbers, same, preferred_element_type=F32).astype(I32)
        slot = iota((8, length), 1) % slots
        return jnp.where(slot < number, first + slot, -1)

    place = places(lambda shape: iota(shape, 1) // slots, count)
    half = count // 2
    place_ref[:8] = places(lambda shape: iota(shape, 1) // slots * 2 + core, half)
    place_ref[8:] = places(lambda shape: iota(shape, 1) // slots * 2 + (1 - core), half)

    compactor = (iota((total, count), 0) == place[:1]).astype(F32).astype(BF)
    raw = jnp.dot(compactor, rows_ref[...], preferred_element_type=F32)
    square = jnp.sum(raw * raw, axis=1, keepdims=True)
    route = jnp.sum(raw * route_ref[...], axis=1, keepdims=True)
    up_part = jnp.dot((raw * gain_ref[...]).astype(BF), w_ref[...], preferred_element_type=F32)
    out_ref[:, :, :hidden_width] = up_part.astype(BF).reshape(parts, chunk, hidden_width)
    square_high = square.astype(BF).astype(F32)
    route_high = route.astype(BF).astype(F32)
    lane = iota((total, 128), 1)
    sums = jnp.where(lane == 0, square_high, 0.0)
    sums = jnp.where(lane == 1, square - square_high, sums)
    sums = jnp.where(lane == 2, route_high, sums)
    sums = jnp.where(lane == 3, route - route_high, sums)
    out_ref[:, :, hidden_width:] = sums.astype(BF).reshape(parts, chunk, 128)


def up_call(core, rows, gain, route, w_up, slots, parts):
    vmem = pl.BlockSpec(memory_space=pltpu.VMEM)
    return pl.pallas_call(
        functools.partial(up_kernel, slots),
        out_shape=(
            jax.ShapeDtypeStruct((parts, ROUTED // parts, w_up.shape[1] + 128), BF),
            jax.ShapeDtypeStruct((16, rows.shape[0] // 2), I32),
        ),
        in_specs=[pl.BlockSpec(memory_space=pltpu.SMEM)] + [vmem] * 4,
        out_specs=(vmem, vmem),
        compiler_params=pltpu.CompilerParams(vmem_limit_bytes=40 * 1024 * 1024),
    )(core.reshape(1), rows, gain, route, w_up)


def per_device(tokens, heavy_index, norm_gain, router, w_up, w_down):
    tok_rows, width = tokens.shape
    slots = heavy_index.shape[0]
    hidden_width = w_up.shape[1]
    chips = lax.axis_size("y")
    parts = lax.axis_size("mp")
    core = lax.axis_index("core")
    used_rows = ROUTED
    chunk = used_rows // parts
    seq_rank = lax.axis_index("y") * 2 + core
    local_index = heavy_index - seq_rank * tok_rows
    token_iota = jnp.arange(tok_rows, dtype=I32)
    picker = (local_index[:, None] == token_iota[None, :]).astype(BF)
    selected = jnp.dot(picker, tokens, preferred_element_type=F32)
    selected = jnp.where(local_index[:, None] >= 0, selected, EMPTY)

    rows = lax.all_gather((selected * SCALE).astype(F16), ("y", "core"), tiled=True)
    rows = (rows.astype(F32) * (1.0 / SCALE)).astype(BF)
    gain = norm_gain[None]
    route = gain * router.astype(F32)[None]
    packed, place = up_call(core, rows, gain, route, w_up, slots, parts)
    own_place, other_place = place[0], place[8]
    packed, own_place, other_place = lax.optimization_barrier((packed, own_place, other_place))
    summed = jnp.sum(lax.all_to_all(packed, "mp", 0, 0, tiled=True).astype(F32), axis=0)
    sums = summed[:, hidden_width:]
    inverse = lax.rsqrt((sums[:, :1] + sums[:, 1:2]) / D + 1e-06)
    scores = jax.nn.sigmoid((sums[:, 2:3] + sums[:, 3:4]) * inverse)
    hidden = jax.nn.gelu(summed[:, :hidden_width] * inverse, approximate=True) * scores
    hidden = jnp.broadcast_to(hidden.astype(BF)[None], (parts, chunk, hidden_width))
    hidden = lax.all_to_all(hidden, "mp", 0, 0, tiled=True).reshape(used_rows, hidden_width)

    row_iota = jnp.arange(used_rows, dtype=I32)

    def wanted(places):
        expander = (places[:, None] == row_iota[None, :]).astype(BF)
        return jnp.dot(expander, hidden, preferred_element_type=F32).astype(BF)

    leave = lax.optimization_barrier(wanted(other_place))
    stay = lax.optimization_barrier(wanted(own_place))
    leave = jnp.dot(leave, w_down, preferred_element_type=F32).astype(BF)
    away = lax.ppermute(leave, "core", [(0, 1), (1, 0)])
    stay = lax.optimization_barrier(jnp.dot(stay, w_down, preferred_element_type=F32))
    chip_sum = (stay + away.astype(F32)).astype(BF).reshape(chips, slots, width)
    targets = jnp.broadcast_to(local_index[None], (chips, slots)).reshape(chips * slots)
    chip_sum, targets = lax.optimization_barrier((chip_sum, targets))
    terms = lax.all_to_all(chip_sum, "y", 0, 0, tiled=True).reshape(chips * slots, width)
    placer = (targets[:, None] == token_iota[None, :]).astype(BF)
    placed = lax.dot_general(
        placer, terms, (((0,), (0,)), ((), ())), preferred_element_type=F32
    )
    return (tokens.astype(F32) + placed).astype(BF)


def solution(mesh):
    dp, seq, mp = mesh.devices.shape
    fine = Mesh(mesh.devices.reshape(dp, seq // 2, 2, mp), ("dp", "y", "core", "mp"))
    seq = ("y", "core")
    rows = ("dp",) + seq
    placed = (P(rows, "mp"), P(rows), P("mp"), P("mp"), P("mp", seq), P(seq, "mp"))
    return jax.shard_map(
        per_device, mesh=fine, in_specs=placed, out_specs=P(rows, "mp"), check_vma=False
    )
```

```python
import functools

import jax
import jax.numpy as jnp
from jax import lax
from jax.experimental import pallas as pl
from jax.experimental.pallas import tpu as pltpu
from jax.sharding import Mesh, PartitionSpec as P

D = 4096
ROUTED = 512
EMPTY = 31.5
LIMIT = 30.5
SCALE = 2048.0
GRANT = 58 * 1024 * 1024
UP_GRANT = 48 * 1024 * 1024
BF = jnp.bfloat16
F16 = jnp.float16
F32 = jnp.float32
I32 = jnp.int32


def iota(shape, axis):
    return lax.broadcasted_iota(I32, shape, axis)


def select_kernel(start_ref, index_hbm, tokens_hbm, out_ref, index_ref, tokens_ref, sems):
    copies = [
        pltpu.make_async_copy(index_hbm, index_ref, sems.at[0]),
        pltpu.make_async_copy(tokens_hbm, tokens_ref, sems.at[1]),
    ]
    for copy in copies:
        copy.start()
    copies[0].wait()
    tok_rows = tokens_ref.shape[0]
    slots = out_ref.shape[0]
    local = index_ref[...] - start_ref[0]
    picker = (iota((tok_rows, slots), 0) == local).astype(F32).astype(BF)
    rows = (((0,), (0,)), ((), ()))
    copies[1].wait()
    selected = lax.dot_general(picker, tokens_ref[...], rows, preferred_element_type=F32)
    unused = ((local < 0) & (iota((8, slots), 0) == 0)).astype(F32).astype(BF)
    mark = jnp.full((8, out_ref.shape[1]), EMPTY, BF)
    selected += lax.dot_general(unused, mark, rows, preferred_element_type=F32)
    out_ref[...] = (selected * SCALE).astype(BF)


def select_call(start, index, tokens):
    vmem = pl.BlockSpec(memory_space=pltpu.VMEM)
    return pl.pallas_call(
        select_kernel,
        out_shape=jax.ShapeDtypeStruct((index.shape[0], tokens.shape[1]), BF),
        in_specs=[pl.BlockSpec(memory_space=pltpu.SMEM)]
        + [pl.BlockSpec(memory_space=pl.ANY)] * 2,
        out_specs=vmem,
        scratch_shapes=[
            pltpu.VMEM((1,) + index.shape, I32),
            pltpu.VMEM(tokens.shape, BF),
            pltpu.SemaphoreType.DMA((2,)),
        ],
        compiler_params=pltpu.CompilerParams(vmem_limit_bytes=GRANT),
    )(start.reshape(1), index.reshape(1, -1), tokens)


def up_kernel(
    slots, core_ref, rows_ref, gain_ref, route_ref, w_hbm, out_ref, place_ref, w_ref, w_sem
):
    w_copy = pltpu.make_async_copy(w_hbm, w_ref, w_sem)
    w_copy.start()
    count = rows_ref.shape[0]
    parts = out_ref.shape[0]
    total = ROUTED
    chunk = total // parts
    hidden_width = w_ref.shape[1]
    core = core_ref[0]
    pick = (iota((8, 128), 1) == 0).astype(BF)
    marks = lax.dot_general(
        pick, rows_ref[:, :128], (((1,), (1,)), ((), ())), preferred_element_type=F32
    )
    used = (marks < LIMIT).astype(F32).astype(BF)
    owner = (iota((count, 128), 0) // slots == iota((count, 128), 1)).astype(BF)
    numbers = jnp.dot(used, owner, preferred_element_type=F32).astype(BF)

    def places(owner_of, length):
        lanes = iota((128, length), 0)
        before = (lanes < owner_of((128, length))).astype(BF)
        same = (lanes == owner_of((128, length))).astype(BF)
        first = jnp.dot(numbers, before, preferred_element_type=F32).astype(I32)
        number = jnp.dot(numbers, same, preferred_element_type=F32).astype(I32)
        slot = iota((8, length), 1) % slots
        return jnp.where(slot < number, first + slot, -1)

    place = places(lambda shape: iota(shape, 1) // slots, count)
    half = count // 2
    place_ref[:8] = places(lambda shape: iota(shape, 1) // slots * 2 + core, half)
    place_ref[8:] = places(lambda shape: iota(shape, 1) // slots * 2 + (1 - core), half)

    compactor = (iota((total, count), 0) == place[:1]).astype(F32).astype(BF)
    raw = jnp.dot(compactor, rows_ref[...], preferred_element_type=F32)
    square = jnp.sum(raw * raw, axis=1, keepdims=True)
    route = jnp.sum(raw * route_ref[...], axis=1, keepdims=True)
    square_high = square.astype(BF).astype(F32)
    route_high = route.astype(BF).astype(F32)
    lane = iota((total, 128), 1)
    sums = jnp.where(lane == 0, square_high, 0.0)
    sums = jnp.where(lane == 1, square - square_high, sums)
    sums = jnp.where(lane == 2, route_high, sums)
    sums = jnp.where(lane == 3, route - route_high, sums)
    sums = jnp.transpose(sums)[:16].astype(BF)
    scaled = (raw * gain_ref[...]).astype(BF)
    w_copy.wait()
    up_part = jnp.dot(scaled, w_ref[...], preferred_element_type=F32)
    out_ref[:, :chunk, :] = up_part.astype(BF).reshape(parts, chunk, hidden_width)
    out_ref[:, chunk:, 128:] = jnp.zeros((parts, 16, hidden_width - 128), BF)
    for m in range(parts):
        out_ref[m, chunk:, :128] = sums[:, m * chunk : (m + 1) * chunk]


def up_call(core, rows, gain, route, w_up, slots, parts):
    vmem = pl.BlockSpec(memory_space=pltpu.VMEM)
    return pl.pallas_call(
        functools.partial(up_kernel, slots),
        out_shape=(
            jax.ShapeDtypeStruct((parts, ROUTED // parts + 16, w_up.shape[1]), BF),
            jax.ShapeDtypeStruct((16, rows.shape[0] // 2), I32),
        ),
        in_specs=[pl.BlockSpec(memory_space=pltpu.SMEM)]
        + [vmem] * 3
        + [pl.BlockSpec(memory_space=pl.ANY)],
        out_specs=(vmem, vmem),
        scratch_shapes=[pltpu.VMEM(w_up.shape, BF), pltpu.SemaphoreType.DMA],
        compiler_params=pltpu.CompilerParams(vmem_limit_bytes=UP_GRANT),
    )(core.reshape(1), rows, gain, route, w_up)


def per_device(tokens, heavy_index, norm_gain, router, w_up, w_down):
    tok_rows, width = tokens.shape
    slots = heavy_index.shape[0]
    hidden_width = w_up.shape[1]
    chips = lax.axis_size("y")
    parts = lax.axis_size("mp")
    core = lax.axis_index("core")
    used_rows = ROUTED
    chunk = used_rows // parts
    seq_rank = lax.axis_index("y") * 2 + core
    local_index = heavy_index - seq_rank * tok_rows
    token_iota = jnp.arange(tok_rows, dtype=I32)
    selected = select_call(seq_rank * tok_rows, heavy_index, tokens)

    rows = lax.all_gather(selected.astype(F16), ("y", "core"), tiled=True)
    rows = (rows.astype(F32) * (1.0 / SCALE)).astype(BF)
    gain = norm_gain[None]
    route = gain * router.astype(F32)[None]
    packed, place = up_call(core, rows, gain, route, w_up, slots, parts)
    own_place, other_place = place[0], place[8]
    packed, own_place, other_place = lax.optimization_barrier((packed, own_place, other_place))
    summed = jnp.sum(lax.all_to_all(packed, "mp", 0, 0, tiled=True).astype(F32), axis=0)
    sums = summed[chunk : chunk + 4, :chunk].T
    inverse = lax.rsqrt((sums[:, :1] + sums[:, 1:2]) / D + 1e-06)
    scores = jax.nn.sigmoid((sums[:, 2:3] + sums[:, 3:4]) * inverse)
    hidden = jax.nn.gelu(summed[:chunk] * inverse, approximate=True) * scores
    hidden = jnp.broadcast_to(hidden.astype(BF)[None], (parts, chunk, hidden_width))
    hidden = lax.all_to_all(hidden, "mp", 0, 0, tiled=True).reshape(used_rows, hidden_width)

    row_iota = jnp.arange(used_rows, dtype=I32)

    def wanted(places):
        expander = (places[:, None] == row_iota[None, :]).astype(BF)
        return jnp.dot(expander, hidden, preferred_element_type=F32).astype(BF)

    leave = lax.optimization_barrier(wanted(other_place))
    stay = lax.optimization_barrier(wanted(own_place))
    leave = jnp.dot(leave, w_down, preferred_element_type=F32).astype(BF)
    away = lax.ppermute(leave, "core", [(0, 1), (1, 0)])
    stay = lax.optimization_barrier(jnp.dot(stay, w_down, preferred_element_type=F32))
    chip_sum = (stay + away.astype(F32)).astype(BF).reshape(chips, slots, width)
    targets = jnp.broadcast_to(local_index[None], (chips, slots)).reshape(chips * slots)
    chip_sum, targets = lax.optimization_barrier((chip_sum, targets))
    terms = lax.all_to_all(chip_sum, "y", 0, 0, tiled=True).reshape(chips * slots, width)
    placer = (targets[:, None] == token_iota[None, :]).astype(BF)
    placed = lax.dot_general(
        placer, terms, (((0,), (0,)), ((), ())), preferred_element_type=F32
    )
    return (tokens.astype(F32) + placed).astype(BF)


def solution(mesh):
    dp, seq, mp = mesh.devices.shape
    fine = Mesh(mesh.devices.reshape(dp, seq // 2, 2, mp), ("dp", "y", "core", "mp"))
    seq = ("y", "core")
    rows = ("dp",) + seq
    placed = (P(rows, "mp"), P(rows), P("mp"), P("mp"), P("mp", seq), P(seq, "mp"))
    return jax.shard_map(
        per_device, mesh=fine, in_specs=placed, out_specs=P(rows, "mp"), check_vma=False
    )
```

```python
import functools

import jax
import jax.numpy as jnp
from jax import lax
from jax.experimental import pallas as pl
from jax.experimental.pallas import tpu as pltpu
from jax.sharding import Mesh, PartitionSpec as P

D = 4096
ROUTED = 512
EMPTY = 31.5
LIMIT = 30.5
SCALE = 2048.0
BF = jnp.bfloat16
F16 = jnp.float16
F32 = jnp.float32
I32 = jnp.int32


def iota(shape, axis):
    return lax.broadcasted_iota(I32, shape, axis)


def up_kernel(slots, core_ref, rows_ref, gain_ref, route_ref, w_ref, out_ref, place_ref):
    count = rows_ref.shape[0]
    parts = out_ref.shape[0]
    total = ROUTED
    chunk = total // parts
    hidden_width = w_ref.shape[1]
    core = core_ref[0]
    pick = (iota((8, 128), 1) == 0).astype(BF)
    marks = lax.dot_general(
        pick, rows_ref[:, :128], (((1,), (1,)), ((), ())), preferred_element_type=F32
    )
    used = (marks < LIMIT).astype(F32).astype(BF)
    owner = (iota((count, 128), 0) // slots == iota((count, 128), 1)).astype(BF)
    numbers = jnp.dot(used, owner, preferred_element_type=F32).astype(BF)

    def owners_of(owner):
        before = (iota((128, owner.shape[1]), 0) < owner).astype(BF)
        same = (iota((128, owner.shape[1]), 0) == owner).astype(BF)
        first = jnp.dot(numbers, before, preferred_element_type=F32).astype(I32)
        return first, jnp.dot(numbers, same, preferred_element_type=F32).astype(I32)

    first, number = owners_of(iota((1, count), 1) // slots)
    slot = iota((8, count), 1) % slots
    row = first + slot
    within = row % chunk
    spot = row - within + row % 2 * (chunk // 2) + within // 2
    spot = jnp.where(slot < number, spot, -1)
    share = slots // 2
    first, number = owners_of(iota((1, count // 2), 1) // share)
    row = first + (first + core) % 2 + 2 * (iota((8, count // 2), 1) % share)
    place_ref[:8] = jnp.where(row < first + number, (row - core) // 2, -1)
    place_ref[8:] = first

    compactor = (iota((total, count), 0) == spot[:1]).astype(F32).astype(BF)
    raw = jnp.dot(compactor, rows_ref[...], preferred_element_type=F32)
    square = jnp.sum(raw * raw, axis=1, keepdims=True)
    route = jnp.sum(raw * route_ref[...], axis=1, keepdims=True)
    square_high = square.astype(BF).astype(F32)
    route_high = route.astype(BF).astype(F32)
    lane = iota((total, 128), 1)
    sums = jnp.where(lane == 0, square_high, 0.0)
    sums = jnp.where(lane == 1, square - square_high, sums)
    sums = jnp.where(lane == 2, route_high, sums)
    sums = jnp.where(lane == 3, route - route_high, sums)
    sums = jnp.transpose(sums)[:16].astype(BF)
    scaled = (raw * gain_ref[...]).astype(BF)
    up_part = jnp.dot(scaled, w_ref[...], preferred_element_type=F32)
    out_ref[:, :chunk, :] = up_part.astype(BF).reshape(parts, chunk, hidden_width)
    out_ref[:, chunk:, 128:] = jnp.zeros((parts, 16, hidden_width - 128), BF)
    for m in range(parts):
        out_ref[m, chunk:, :128] = sums[:, m * chunk : (m + 1) * chunk]


def up_call(core, rows, gain, route, w_up, slots, parts):
    vmem = pl.BlockSpec(memory_space=pltpu.VMEM)
    return pl.pallas_call(
        functools.partial(up_kernel, slots),
        out_shape=(
            jax.ShapeDtypeStruct((parts, ROUTED // parts + 16, w_up.shape[1]), BF),
            jax.ShapeDtypeStruct((16, rows.shape[0] // 2), I32),
        ),
        in_specs=[pl.BlockSpec(memory_space=pltpu.SMEM)] + [vmem] * 4,
        out_specs=(vmem, vmem),
        compiler_params=pltpu.CompilerParams(vmem_limit_bytes=40 * 1024 * 1024),
    )(core.reshape(1), rows, gain, route, w_up)


def per_device(tokens, heavy_index, norm_gain, router, w_up, w_down):
    tok_rows, width = tokens.shape
    slots = heavy_index.shape[0]
    hidden_width = w_up.shape[1]
    chips = lax.axis_size("y")
    parts = lax.axis_size("mp")
    core = lax.axis_index("core")
    used_rows = ROUTED
    share = slots // 2
    chunk = used_rows // parts
    seq_rank = lax.axis_index("y") * 2 + core
    local_index = heavy_index - seq_rank * tok_rows
    token_iota = jnp.arange(tok_rows, dtype=I32)
    picker = (local_index[:, None] == token_iota[None, :]).astype(BF)
    selected = jnp.dot(picker, tokens, preferred_element_type=F32)
    selected = jnp.where(local_index[:, None] >= 0, selected, EMPTY)

    rows = lax.all_gather((selected * SCALE).astype(F16), ("y", "core"), tiled=True)
    rows = (rows.astype(F32) * (1.0 / SCALE)).astype(BF)
    gain = norm_gain[None]
    route = gain * router.astype(F32)[None]
    packed, place = up_call(core, rows, gain, route, w_up, slots, parts)
    mine, start = place[0], lax.dynamic_index_in_dim(place[8], seq_rank * share, keepdims=False)
    pairs = local_index.reshape(share, 2).T
    targets = jnp.where(start % 2 == 0, pairs, pairs[::-1])
    targets = jnp.broadcast_to(targets[None], (chips, 2, share)).reshape(chips * slots)
    packed, mine, targets = lax.optimization_barrier((packed, mine, targets))
    summed = jnp.sum(lax.all_to_all(packed, "mp", 0, 0, tiled=True).astype(F32), axis=0)
    sums = summed[chunk : chunk + 4, :chunk].T
    inverse = lax.rsqrt((sums[:, :1] + sums[:, 1:2]) / D + 1e-06)
    scores = jax.nn.sigmoid((sums[:, 2:3] + sums[:, 3:4]) * inverse)
    hidden = jax.nn.gelu(summed[:chunk] * inverse, approximate=True) * scores
    hidden = hidden.astype(BF).reshape(2, 1, chunk // 2, hidden_width)
    hidden = jnp.broadcast_to(hidden, (2, parts, chunk // 2, hidden_width))
    hidden = lax.all_to_all(
        hidden.reshape(2 * parts, chunk // 2, hidden_width), ("core", "mp"), 0, 0, tiled=True
    ).reshape(2, used_rows // 2, hidden_width)
    w_near = lax.ppermute(w_down, "core", [(0, 1), (1, 0)])
    here = jnp.where(core == 0, hidden[0], hidden[1])
    near = jnp.where(core == 0, hidden[1], hidden[0])

    expander = (mine[:, None] == jnp.arange(used_rows // 2, dtype=I32)[None, :]).astype(BF)
    wanted = jnp.dot(
        expander, jnp.concatenate([here, near], axis=1), preferred_element_type=F32
    ).astype(BF)
    wanted = lax.optimization_barrier(wanted)
    down = jnp.dot(wanted[:, :hidden_width], w_down, preferred_element_type=F32)
    down += jnp.dot(wanted[:, hidden_width:], w_near, preferred_element_type=F32)
    chip_sum = down.astype(BF).reshape(2 * chips, share, width)
    terms = lax.all_to_all(chip_sum, ("y", "core"), 0, 0, tiled=True).reshape(-1, width)
    placer = (targets[:, None] == token_iota[None, :]).astype(BF)
    placed = lax.dot_general(
        placer, terms, (((0,), (0,)), ((), ())), preferred_element_type=F32
    )
    return (tokens.astype(F32) + placed).astype(BF)


def solution(mesh):
    dp, seq, mp = mesh.devices.shape
    fine = Mesh(mesh.devices.reshape(dp, seq // 2, 2, mp), ("dp", "y", "core", "mp"))
    seq = ("y", "core")
    rows = ("dp",) + seq
    placed = (P(rows, "mp"), P(rows), P("mp"), P("mp"), P("mp", seq), P(seq, "mp"))
    return jax.shard_map(
        per_device, mesh=fine, in_specs=placed, out_specs=P(rows, "mp"), check_vma=False
    )
```

```python
import functools

import jax
import jax.numpy as jnp
from jax import lax
from jax.experimental import pallas as pl
from jax.experimental.pallas import tpu as pltpu
from jax.sharding import Mesh, PartitionSpec as P

D = 4096
ROUTED = 512
EMPTY = 31.5
LIMIT = 30.5
SCALE = 2048.0
BF = jnp.bfloat16
F16 = jnp.float16
F32 = jnp.float32
I32 = jnp.int32


def iota(shape, axis):
    return lax.broadcasted_iota(I32, shape, axis)


def up_kernel(
    slots, core_ref, rank_ref, rows_ref, gain_ref, route_ref, w_ref, out_ref, place_ref
):
    count = rows_ref.shape[0]
    parts = out_ref.shape[0]
    total = ROUTED
    chunk = total // parts
    hidden_width = w_ref.shape[1]
    core, seq_rank = core_ref[0], rank_ref[0]
    pick = (iota((8, 128), 1) == 0).astype(BF)
    marks = lax.dot_general(
        pick, rows_ref[:, :128], (((1,), (1,)), ((), ())), preferred_element_type=F32
    )
    used = (marks < LIMIT).astype(F32).astype(BF)
    owner = (iota((count, 128), 0) // slots == iota((count, 128), 1)).astype(BF)
    numbers = jnp.dot(used, owner, preferred_element_type=F32).astype(BF)

    def owners_of(owner):
        before = (iota((128, owner.shape[1]), 0) < owner).astype(BF)
        same = (iota((128, owner.shape[1]), 0) == owner).astype(BF)
        first = jnp.dot(numbers, before, preferred_element_type=F32).astype(I32)
        return first, jnp.dot(numbers, same, preferred_element_type=F32).astype(I32)

    first, number = owners_of(iota((1, count), 1) // slots)
    slot = iota((8, count), 1) % slots
    row = first + slot
    within = row % chunk
    spot = row - within + row % 2 * (chunk // 2) + within // 2
    spot = jnp.where(slot < number, spot, -1)
    share = slots // 2
    first, number = owners_of(iota((1, count // 2), 1) // share)
    row = first + (first + core) % 2 + 2 * (iota((8, count // 2), 1) % share)
    place_ref[:8] = jnp.where(row < first + number, (row - core) // 2, -1)
    place_ref[8:] = owners_of(jnp.full((1, count // 2), seq_rank, I32))[0]

    compactor = (iota((total, count), 0) == spot[:1]).astype(F32).astype(BF)
    raw = jnp.dot(compactor, rows_ref[...], preferred_element_type=F32)
    square = jnp.sum(raw * raw, axis=1, keepdims=True)
    route = jnp.sum(raw * route_ref[...], axis=1, keepdims=True)
    square_high = square.astype(BF).astype(F32)
    route_high = route.astype(BF).astype(F32)
    lane = iota((total, 128), 1)
    sums = jnp.where(lane == 0, square_high, 0.0)
    sums = jnp.where(lane == 1, square - square_high, sums)
    sums = jnp.where(lane == 2, route_high, sums)
    sums = jnp.where(lane == 3, route - route_high, sums)
    sums = jnp.transpose(sums)[:16].astype(BF)
    scaled = (raw * gain_ref[...]).astype(BF)
    up_part = jnp.dot(scaled, w_ref[...], preferred_element_type=F32)
    out_ref[:, :chunk, :] = up_part.astype(BF).reshape(parts, chunk, hidden_width)
    out_ref[:, chunk:, 128:] = jnp.zeros((parts, 16, hidden_width - 128), BF)
    for m in range(parts):
        out_ref[m, chunk:, :128] = sums[:, m * chunk : (m + 1) * chunk]


def up_call(core, seq_rank, rows, gain, route, w_up, slots, parts):
    vmem = pl.BlockSpec(memory_space=pltpu.VMEM)
    return pl.pallas_call(
        functools.partial(up_kernel, slots),
        out_shape=(
            jax.ShapeDtypeStruct((parts, ROUTED // parts + 16, w_up.shape[1]), BF),
            jax.ShapeDtypeStruct((16, rows.shape[0] // 2), I32),
        ),
        in_specs=[pl.BlockSpec(memory_space=pltpu.SMEM)] * 2 + [vmem] * 4,
        out_specs=(vmem, vmem),
        compiler_params=pltpu.CompilerParams(vmem_limit_bytes=40 * 1024 * 1024),
    )(core.reshape(1), seq_rank.reshape(1), rows, gain, route, w_up)


def per_device(tokens, heavy_index, norm_gain, router, w_up, w_down):
    tok_rows, width = tokens.shape
    slots = heavy_index.shape[0]
    hidden_width = w_up.shape[1]
    chips = lax.axis_size("y")
    parts = lax.axis_size("mp")
    core = lax.axis_index("core")
    used_rows = ROUTED
    share = slots // 2
    chunk = used_rows // parts
    seq_rank = lax.axis_index("y") * 2 + core
    local_index = heavy_index - seq_rank * tok_rows
    token_iota = jnp.arange(tok_rows, dtype=I32)
    picker = (local_index[:, None] == token_iota[None, :]).astype(BF)
    selected = jnp.dot(picker, tokens, preferred_element_type=F32)
    selected = jnp.where(local_index[:, None] >= 0, selected, EMPTY)

    rows = lax.all_gather((selected * SCALE).astype(F16), ("y", "core"), tiled=True)
    rows = (rows.astype(F32) * (1.0 / SCALE)).astype(BF)
    gain = norm_gain[None]
    route = gain * router.astype(F32)[None]
    packed, place = up_call(core, seq_rank, rows, gain, route, w_up, slots, parts)
    packed = lax.all_to_all(packed, "mp", 0, 0, tiled=True)
    packed, place, local_index = lax.optimization_barrier((packed, place, local_index))
    mine, start = place[0], place[8]
    pairs = local_index.reshape(share, 2).T
    evens = jnp.broadcast_to(pairs[None], (chips, 2, share)).reshape(chips * slots)
    odds = jnp.broadcast_to(pairs[None, ::-1], (chips, 2, share)).reshape(chips * slots)
    targets = jnp.where(start % 2 == 0, evens, odds)
    summed = jnp.sum(packed.astype(F32), axis=0)
    sums = summed[chunk : chunk + 4, :chunk].T
    inverse = lax.rsqrt((sums[:, :1] + sums[:, 1:2]) / D + 1e-06)
    scores = jax.nn.sigmoid((sums[:, 2:3] + sums[:, 3:4]) * inverse)
    hidden = jax.nn.gelu(summed[:chunk] * inverse, approximate=True) * scores
    hidden = hidden.astype(BF).reshape(2, 1, chunk // 2, hidden_width)
    hidden = jnp.broadcast_to(hidden, (2, parts, chunk // 2, hidden_width))
    hidden = lax.all_to_all(
        hidden.reshape(2 * parts, chunk // 2, hidden_width), ("core", "mp"), 0, 0, tiled=True
    ).reshape(2, used_rows // 2, hidden_width)
    hidden, targets = lax.optimization_barrier((hidden, targets))
    w_near = lax.ppermute(w_down, "core", [(0, 1), (1, 0)])
    here = jnp.where(core == 0, hidden[0], hidden[1])
    near = jnp.where(core == 0, hidden[1], hidden[0])

    expander = (mine[:, None] == jnp.arange(used_rows // 2, dtype=I32)[None, :]).astype(BF)
    wanted = jnp.dot(
        expander, jnp.concatenate([here, near], axis=1), preferred_element_type=F32
    ).astype(BF)
    wanted = lax.optimization_barrier(wanted)
    down = jnp.dot(wanted[:, :hidden_width], w_down, preferred_element_type=F32)
    down += jnp.dot(wanted[:, hidden_width:], w_near, preferred_element_type=F32)
    chip_sum = down.astype(BF).reshape(2 * chips, share, width)
    terms = lax.all_to_all(chip_sum, ("y", "core"), 0, 0, tiled=True).reshape(-1, width)
    placer = (targets[:, None] == token_iota[None, :]).astype(BF)
    placed = lax.dot_general(
        placer, terms, (((0,), (0,)), ((), ())), preferred_element_type=F32
    )
    return (tokens.astype(F32) + placed).astype(BF)


def solution(mesh):
    dp, seq, mp = mesh.devices.shape
    fine = Mesh(mesh.devices.reshape(dp, seq // 2, 2, mp), ("dp", "y", "core", "mp"))
    seq = ("y", "core")
    rows = ("dp",) + seq
    placed = (P(rows, "mp"), P(rows), P("mp"), P("mp"), P("mp", seq), P(seq, "mp"))
    return jax.shard_map(
        per_device, mesh=fine, in_specs=placed, out_specs=P(rows, "mp"), check_vma=False
    )
```

```python
import functools

import jax
import jax.numpy as jnp
from jax import lax
from jax.experimental import pallas as pl
from jax.experimental.pallas import tpu as pltpu
from jax.sharding import Mesh, PartitionSpec as P

D = 4096
ROUTED = 512
EMPTY = 31.5
LIMIT = 30.5
SCALE = 2048.0
BF = jnp.bfloat16
F16 = jnp.float16
F32 = jnp.float32
I32 = jnp.int32


def iota(shape, axis):
    return lax.broadcasted_iota(I32, shape, axis)


def up_kernel(
    slots, core_ref, rank_ref, rows_ref, gain_ref, route_ref, w_ref, out_ref, place_ref
):
    count = rows_ref.shape[0]
    parts = out_ref.shape[0]
    total = ROUTED
    chunk = total // parts
    hidden_width = w_ref.shape[1]
    core, seq_rank = core_ref[0], rank_ref[0]
    pick = (iota((8, 128), 1) == 0).astype(BF)
    marks = lax.dot_general(
        pick, rows_ref[:, :128], (((1,), (1,)), ((), ())), preferred_element_type=F32
    )
    used = (marks < LIMIT).astype(F32).astype(BF)
    owner = (iota((count, 128), 0) // slots == iota((count, 128), 1)).astype(BF)
    numbers = jnp.dot(used, owner, preferred_element_type=F32).astype(BF)

    def owners_of(owner):
        before = (iota((128, owner.shape[1]), 0) < owner).astype(BF)
        same = (iota((128, owner.shape[1]), 0) == owner).astype(BF)
        first = jnp.dot(numbers, before, preferred_element_type=F32).astype(I32)
        return first, jnp.dot(numbers, same, preferred_element_type=F32).astype(I32)

    first, number = owners_of(iota((1, count), 1) // slots)
    slot = iota((8, count), 1) % slots
    row = first + slot
    within = row % chunk
    spot = row - within + row % 2 * (chunk // 2) + within // 2
    spot = jnp.where(slot < number, spot, -1)
    share = slots // 2
    first, number = owners_of(iota((1, count // 2), 1) // share)
    row = first + (first + core) % 2 + 2 * (iota((8, count // 2), 1) % share)
    place_ref[:8] = jnp.where(row < first + number, (row - core) // 2, -1)
    place_ref[8:] = owners_of(jnp.full((1, count // 2), seq_rank, I32))[0]

    compactor = (iota((total, count), 0) == spot[:1]).astype(F32).astype(BF)
    raw = jnp.dot(compactor, rows_ref[...], preferred_element_type=F32)
    square = jnp.sum(raw * raw, axis=1, keepdims=True)
    route = jnp.sum(raw * route_ref[...], axis=1, keepdims=True)
    square_high = square.astype(BF).astype(F32)
    route_high = route.astype(BF).astype(F32)
    lane = iota((total, 128), 1)
    sums = jnp.where(lane == 0, square_high, 0.0)
    sums = jnp.where(lane == 1, square - square_high, sums)
    sums = jnp.where(lane == 2, route_high, sums)
    sums = jnp.where(lane == 3, route - route_high, sums)
    sums = jnp.transpose(sums)[:16].astype(BF)
    scaled = (raw * gain_ref[...]).astype(BF)
    up_part = jnp.dot(scaled, w_ref[...], preferred_element_type=F32)
    out_ref[:, :chunk, :] = up_part.astype(BF).reshape(parts, chunk, hidden_width)
    out_ref[:, chunk:, 128:] = jnp.zeros((parts, 16, hidden_width - 128), BF)
    for m in range(parts):
        out_ref[m, chunk:, :128] = sums[:, m * chunk : (m + 1) * chunk]


def up_call(core, seq_rank, rows, gain, route, w_up, slots, parts):
    vmem = pl.BlockSpec(memory_space=pltpu.VMEM)
    return pl.pallas_call(
        functools.partial(up_kernel, slots),
        out_shape=(
            jax.ShapeDtypeStruct((parts, ROUTED // parts + 16, w_up.shape[1]), BF),
            jax.ShapeDtypeStruct((16, rows.shape[0] // 2), I32),
        ),
        in_specs=[pl.BlockSpec(memory_space=pltpu.SMEM)] * 2 + [vmem] * 4,
        out_specs=(vmem, vmem),
        compiler_params=pltpu.CompilerParams(vmem_limit_bytes=40 * 1024 * 1024),
    )(core.reshape(1), seq_rank.reshape(1), rows, gain, route, w_up)


def gelu_kernel(packed_ref, out_ref):
    parts, height, hidden_width = packed_ref.shape
    chunk = height - 16
    summed = packed_ref[0].astype(F32)
    for m in range(1, parts):
        summed += packed_ref[m].astype(F32)
    sums = jnp.transpose(summed[chunk:, :chunk])
    inverse = lax.rsqrt((sums[:, :1] + sums[:, 1:2]) / D + 1e-06)
    scores = jax.nn.sigmoid((sums[:, 2:3] + sums[:, 3:4]) * inverse)
    hidden = jax.nn.gelu(summed[:chunk] * inverse, approximate=True) * scores
    hidden = hidden.astype(BF)
    half = chunk // 2
    for side in range(2):
        for m in range(parts):
            out_ref[side * parts + m] = hidden[side * half : (side + 1) * half]


def gelu_call(packed):
    parts, height, hidden_width = packed.shape
    vmem = pl.BlockSpec(memory_space=pltpu.VMEM)
    return pl.pallas_call(
        gelu_kernel,
        out_shape=jax.ShapeDtypeStruct((2 * parts, (height - 16) // 2, hidden_width), BF),
        in_specs=[vmem],
        out_specs=vmem,
        compiler_params=pltpu.CompilerParams(vmem_limit_bytes=32 * 1024 * 1024),
    )(packed)


def place_kernel(targets_ref, terms_ref, tokens_ref, out_ref):
    shape = (tokens_ref.shape[0], terms_ref.shape[0])
    placer = (iota(shape, 0) == targets_ref[...]).astype(F32).astype(BF)
    placed = jnp.dot(placer, terms_ref[...], preferred_element_type=F32)
    out_ref[...] = (tokens_ref[...].astype(F32) + placed).astype(BF)


def place_call(targets, terms, tokens):
    count, width = terms.shape
    block = width // 2
    return pl.pallas_call(
        place_kernel,
        out_shape=jax.ShapeDtypeStruct(tokens.shape, BF),
        grid=(2,),
        in_specs=[
            pl.BlockSpec((1, count), lambda i: (0, 0)),
            pl.BlockSpec((count, block), lambda i: (0, i)),
            pl.BlockSpec((tokens.shape[0], block), lambda i: (0, i)),
        ],
        out_specs=pl.BlockSpec((tokens.shape[0], block), lambda i: (0, i)),
        compiler_params=pltpu.CompilerParams(vmem_limit_bytes=32 * 1024 * 1024),
    )(targets.reshape(1, -1), terms, tokens)


def per_device(tokens, heavy_index, norm_gain, router, w_up, w_down):
    tok_rows, width = tokens.shape
    slots = heavy_index.shape[0]
    hidden_width = w_up.shape[1]
    chips = lax.axis_size("y")
    parts = lax.axis_size("mp")
    core = lax.axis_index("core")
    used_rows = ROUTED
    share = slots // 2
    seq_rank = lax.axis_index("y") * 2 + core
    local_index = heavy_index - seq_rank * tok_rows
    token_iota = jnp.arange(tok_rows, dtype=I32)
    picker = (local_index[:, None] == token_iota[None, :]).astype(BF)
    selected = jnp.dot(picker, tokens, preferred_element_type=F32)
    selected = jnp.where(local_index[:, None] >= 0, selected, EMPTY)

    rows = lax.all_gather((selected * SCALE).astype(F16), ("y", "core"), tiled=True)
    rows = (rows.astype(F32) * (1.0 / SCALE)).astype(BF)
    gain = norm_gain[None]
    route = gain * router.astype(F32)[None]
    packed, place = up_call(core, seq_rank, rows, gain, route, w_up, slots, parts)
    packed = lax.all_to_all(packed, "mp", 0, 0, tiled=True)
    packed, place, local_index = lax.optimization_barrier((packed, place, local_index))
    mine, start = place[0], place[8]
    pairs = local_index.reshape(share, 2).T
    evens = jnp.broadcast_to(pairs[None], (chips, 2, share)).reshape(chips * slots)
    odds = jnp.broadcast_to(pairs[None, ::-1], (chips, 2, share)).reshape(chips * slots)
    targets = jnp.where(start % 2 == 0, evens, odds)
    hidden = lax.all_to_all(
        gelu_call(packed), ("core", "mp"), 0, 0, tiled=True
    ).reshape(2, used_rows // 2, hidden_width)
    hidden, targets = lax.optimization_barrier((hidden, targets))
    w_near = lax.ppermute(w_down, "core", [(0, 1), (1, 0)])
    here = jnp.where(core == 0, hidden[0], hidden[1])
    near = jnp.where(core == 0, hidden[1], hidden[0])

    expander = (mine[:, None] == jnp.arange(used_rows // 2, dtype=I32)[None, :]).astype(BF)
    wanted = jnp.dot(
        expander, jnp.concatenate([here, near], axis=1), preferred_element_type=F32
    ).astype(BF)
    wanted = lax.optimization_barrier(wanted)
    down = jnp.dot(wanted[:, :hidden_width], w_down, preferred_element_type=F32)
    down += jnp.dot(wanted[:, hidden_width:], w_near, preferred_element_type=F32)
    chip_sum = down.astype(BF).reshape(2 * chips, share, width)
    terms = lax.all_to_all(chip_sum, ("y", "core"), 0, 0, tiled=True).reshape(-1, width)
    return place_call(targets, terms, tokens)


def solution(mesh):
    dp, seq, mp = mesh.devices.shape
    fine = Mesh(mesh.devices.reshape(dp, seq // 2, 2, mp), ("dp", "y", "core", "mp"))
    seq = ("y", "core")
    rows = ("dp",) + seq
    placed = (P(rows, "mp"), P(rows), P("mp"), P("mp"), P("mp", seq), P(seq, "mp"))
    return jax.shard_map(
        per_device, mesh=fine, in_specs=placed, out_specs=P(rows, "mp"), check_vma=False
    )
```

```python
import functools

import jax
import jax.numpy as jnp
from jax import lax
from jax.experimental import pallas as pl
from jax.experimental.pallas import tpu as pltpu
from jax.sharding import Mesh, PartitionSpec as P

D = 4096
ROUTED = 512
EMPTY = 31.5
LIMIT = 30.5
SCALE = 2048.0
BF = jnp.bfloat16
F16 = jnp.float16
F32 = jnp.float32
I32 = jnp.int32


def iota(shape, axis):
    return lax.broadcasted_iota(I32, shape, axis)


def up_kernel(
    slots, tok_rows, core_ref, rank_ref, index_ref, rows_ref, gain_ref, route_ref, w_ref, out_ref, place_ref
):
    count = rows_ref.shape[0]
    parts = out_ref.shape[0]
    total = ROUTED
    chunk = total // parts
    hidden_width = w_ref.shape[1]
    core, seq_rank = core_ref[0], rank_ref[0]
    pick = (iota((8, 128), 1) == 0).astype(BF)
    marks = lax.dot_general(
        pick, rows_ref[:, :128], (((1,), (1,)), ((), ())), preferred_element_type=F32
    )
    used = (marks < LIMIT).astype(F32).astype(BF)
    owner = (iota((count, 128), 0) // slots == iota((count, 128), 1)).astype(BF)
    numbers = jnp.dot(used, owner, preferred_element_type=F32).astype(BF)

    def owners_of(owner):
        before = (iota((128, owner.shape[1]), 0) < owner).astype(BF)
        same = (iota((128, owner.shape[1]), 0) == owner).astype(BF)
        first = jnp.dot(numbers, before, preferred_element_type=F32).astype(I32)
        return first, jnp.dot(numbers, same, preferred_element_type=F32).astype(I32)

    first, number = owners_of(iota((1, count), 1) // slots)
    slot = iota((8, count), 1) % slots
    row = first + slot
    within = row % chunk
    spot = row - within + row % 2 * (chunk // 2) + within // 2
    spot = jnp.where(slot < number, spot, -1)
    share = slots // 2
    first, number = owners_of(iota((1, count // 2), 1) // share)
    row = first + (first + core) % 2 + 2 * (iota((8, count // 2), 1) % share)
    place_ref[:8] = jnp.where(row < first + number, (row - core) // 2, -1)
    start = owners_of(jnp.full((1, count // 2), seq_rank, I32))[0]
    lanes = iota((1, count // 2), 1)
    sent = 2 * (lanes % share) + (start[:1] + lanes // share) % 2
    chosen = (iota((slots, count // 2), 0) == sent).astype(F32).astype(BF)
    local = index_ref[...] - seq_rank * tok_rows
    local = jnp.broadcast_to(jnp.where(local < 0, -1, local), (8, slots))
    upper = (local >> 7).astype(F32).astype(BF)
    lower = (local & 127).astype(F32).astype(BF)
    target = 128.0 * jnp.dot(upper, chosen, preferred_element_type=F32)
    target += jnp.dot(lower, chosen, preferred_element_type=F32)
    place_ref[8:] = target.astype(I32)

    compactor = (iota((total, count), 0) == spot[:1]).astype(F32).astype(BF)
    raw = jnp.dot(compactor, rows_ref[...], preferred_element_type=F32)
    square = jnp.sum(raw * raw, axis=1, keepdims=True)
    route = jnp.sum(raw * route_ref[...], axis=1, keepdims=True)
    square_high = square.astype(BF).astype(F32)
    route_high = route.astype(BF).astype(F32)
    lane = iota((total, 128), 1)
    sums = jnp.where(lane == 0, square_high, 0.0)
    sums = jnp.where(lane == 1, square - square_high, sums)
    sums = jnp.where(lane == 2, route_high, sums)
    sums = jnp.where(lane == 3, route - route_high, sums)
    sums = jnp.transpose(sums)[:16].astype(BF)
    scaled = (raw * gain_ref[...]).astype(BF)
    up_part = jnp.dot(scaled, w_ref[...], preferred_element_type=F32)
    out_ref[:, :chunk, :] = up_part.astype(BF).reshape(parts, chunk, hidden_width)
    out_ref[:, chunk:, 128:] = jnp.zeros((parts, 16, hidden_width - 128), BF)
    for m in range(parts):
        out_ref[m, chunk:, :128] = sums[:, m * chunk : (m + 1) * chunk]


def up_call(core, seq_rank, index, tok_rows, rows, gain, route, w_up, slots, parts):
    vmem = pl.BlockSpec(memory_space=pltpu.VMEM)
    return pl.pallas_call(
        functools.partial(up_kernel, slots, tok_rows),
        out_shape=(
            jax.ShapeDtypeStruct((parts, ROUTED // parts + 16, w_up.shape[1]), BF),
            jax.ShapeDtypeStruct((16, rows.shape[0] // 2), I32),
        ),
        in_specs=[pl.BlockSpec(memory_space=pltpu.SMEM)] * 2 + [vmem] * 5,
        out_specs=(vmem, vmem),
        compiler_params=pltpu.CompilerParams(vmem_limit_bytes=40 * 1024 * 1024),
    )(core.reshape(1), seq_rank.reshape(1), index.reshape(1, -1), rows, gain, route, w_up)


def per_device(tokens, heavy_index, norm_gain, router, w_up, w_down):
    tok_rows, width = tokens.shape
    slots = heavy_index.shape[0]
    hidden_width = w_up.shape[1]
    chips = lax.axis_size("y")
    parts = lax.axis_size("mp")
    core = lax.axis_index("core")
    used_rows = ROUTED
    share = slots // 2
    chunk = used_rows // parts
    seq_rank = lax.axis_index("y") * 2 + core
    local_index = heavy_index - seq_rank * tok_rows
    token_iota = jnp.arange(tok_rows, dtype=I32)
    picker = (local_index[:, None] == token_iota[None, :]).astype(BF)
    selected = jnp.dot(picker, tokens, preferred_element_type=F32)
    selected = jnp.where(local_index[:, None] >= 0, selected, EMPTY)

    rows = lax.all_gather((selected * SCALE).astype(F16), ("y", "core"), tiled=True)
    rows, w_here = lax.optimization_barrier((rows, w_down))
    w_near = lax.ppermute(w_here, "core", [(0, 1), (1, 0)])
    rows = (rows.astype(F32) * (1.0 / SCALE)).astype(BF)
    gain = norm_gain[None]
    route = gain * router.astype(F32)[None]
    packed, place = up_call(
        core, seq_rank, heavy_index, tok_rows, rows, gain, route, w_up, slots, parts
    )
    lower_core = jnp.broadcast_to(core == 0, (1, 1))
    packed, mine, targets, lower_core = lax.optimization_barrier(
        (packed, place[0], place[8], lower_core)
    )
    packed = lax.all_to_all(packed, "mp", 0, 0, tiled=True)
    packed, w_near = lax.optimization_barrier((packed, w_near))
    summed = jnp.sum(packed.astype(F32), axis=0)
    sums = summed[chunk : chunk + 4, :chunk].T
    inverse = lax.rsqrt((sums[:, :1] + sums[:, 1:2]) / D + 1e-06)
    scores = jax.nn.sigmoid((sums[:, 2:3] + sums[:, 3:4]) * inverse)
    hidden = jax.nn.gelu(summed[:chunk] * inverse, approximate=True) * scores
    hidden = hidden.astype(BF).reshape(2, 1, chunk // 2, hidden_width)
    hidden = jnp.broadcast_to(hidden, (2, parts, chunk // 2, hidden_width))
    hidden = lax.all_to_all(
        hidden.reshape(2 * parts, chunk // 2, hidden_width), ("core", "mp"), 0, 0, tiled=True
    ).reshape(2, used_rows // 2, hidden_width)
    here = jnp.where(lower_core, hidden[0], hidden[1])
    near = jnp.where(lower_core, hidden[1], hidden[0])

    expander = (mine[:, None] == jnp.arange(used_rows // 2, dtype=I32)[None, :]).astype(BF)
    wanted = jnp.dot(
        expander, jnp.concatenate([here, near], axis=1), preferred_element_type=F32
    ).astype(BF)
    wanted = lax.optimization_barrier(wanted)
    down = jnp.dot(wanted[:, :hidden_width], w_down, preferred_element_type=F32)
    down += jnp.dot(wanted[:, hidden_width:], w_near, preferred_element_type=F32)
    chip_sum = down.astype(BF).reshape(2 * chips, share, width)
    terms = lax.all_to_all(chip_sum, ("y", "core"), 0, 0, tiled=True).reshape(-1, width)
    placer = (targets[:, None] == token_iota[None, :]).astype(BF)
    placed = lax.dot_general(
        placer, terms, (((0,), (0,)), ((), ())), preferred_element_type=F32
    )
    return (tokens.astype(F32) + placed).astype(BF)


def solution(mesh):
    dp, seq, mp = mesh.devices.shape
    fine = Mesh(mesh.devices.reshape(dp, seq // 2, 2, mp), ("dp", "y", "core", "mp"))
    seq = ("y", "core")
    rows = ("dp",) + seq
    placed = (P(rows, "mp"), P(rows), P("mp"), P("mp"), P("mp", seq), P(seq, "mp"))
    return jax.shard_map(
        per_device, mesh=fine, in_specs=placed, out_specs=P(rows, "mp"), check_vma=False
    )
```

```python
import functools

import jax
import jax.numpy as jnp
from jax import lax
from jax.experimental import pallas as pl
from jax.experimental.pallas import tpu as pltpu
from jax.sharding import Mesh, PartitionSpec as P

D = 4096
ROUTED = 512
EMPTY = 31.5
LIMIT = 30.5
SCALE = 2048.0
BF = jnp.bfloat16
F16 = jnp.float16
F32 = jnp.float32
I32 = jnp.int32


def iota(shape, axis):
    return lax.broadcasted_iota(I32, shape, axis)


def up_kernel(
    slots, core_ref, rank_ref, rows_ref, gain_ref, route_ref, w_ref, out_ref, place_ref
):
    count = rows_ref.shape[0]
    parts = out_ref.shape[0]
    total = ROUTED
    chunk = total // parts
    hidden_width = w_ref.shape[1]
    core, seq_rank = core_ref[0], rank_ref[0]
    pick = (iota((8, 128), 1) == 0).astype(BF)
    marks = lax.dot_general(
        pick, rows_ref[:, :128], (((1,), (1,)), ((), ())), preferred_element_type=F32
    )
    used = (marks < LIMIT).astype(F32).astype(BF)
    owner = (iota((count, 128), 0) // slots == iota((count, 128), 1)).astype(BF)
    numbers = jnp.dot(used, owner, preferred_element_type=F32).astype(BF)

    def owners_of(owner):
        before = (iota((128, owner.shape[1]), 0) < owner).astype(BF)
        same = (iota((128, owner.shape[1]), 0) == owner).astype(BF)
        first = jnp.dot(numbers, before, preferred_element_type=F32).astype(I32)
        return first, jnp.dot(numbers, same, preferred_element_type=F32).astype(I32)

    first, number = owners_of(iota((1, count), 1) // slots)
    slot = iota((8, count), 1) % slots
    row = first + slot
    within = row % chunk
    spot = row - within + row % 2 * (chunk // 2) + within // 2
    spot = jnp.where(slot < number, spot, -1)
    share = slots // 2
    first, number = owners_of(iota((1, count // 2), 1) // share)
    row = first + (first + core) % 2 + 2 * (iota((8, count // 2), 1) % share)
    place_ref[:8] = jnp.where(row < first + number, (row - core) // 2, -1)
    place_ref[8:] = owners_of(jnp.full((1, count // 2), seq_rank, I32))[0]

    compactor = (iota((total, count), 0) == spot[:1]).astype(F32).astype(BF)
    raw = jnp.dot(compactor, rows_ref[...], preferred_element_type=F32)
    square = jnp.sum(raw * raw, axis=1, keepdims=True)
    route = jnp.sum(raw * route_ref[...], axis=1, keepdims=True)
    square_high = square.astype(BF).astype(F32)
    route_high = route.astype(BF).astype(F32)
    lane = iota((total, 128), 1)
    sums = jnp.where(lane == 0, square_high, 0.0)
    sums = jnp.where(lane == 1, square - square_high, sums)
    sums = jnp.where(lane == 2, route_high, sums)
    sums = jnp.where(lane == 3, route - route_high, sums)
    sums = jnp.transpose(sums)[:16].astype(BF)
    scaled = (raw * gain_ref[...]).astype(BF)
    up_part = jnp.dot(scaled, w_ref[...], preferred_element_type=F32)
    out_ref[:, :chunk, :] = up_part.astype(BF).reshape(parts, chunk, hidden_width)
    out_ref[:, chunk:, 128:] = jnp.zeros((parts, 16, hidden_width - 128), BF)
    for m in range(parts):
        out_ref[m, chunk:, :128] = sums[:, m * chunk : (m + 1) * chunk]


def up_call(core, seq_rank, rows, gain, route, w_up, slots, parts):
    vmem = pl.BlockSpec(memory_space=pltpu.VMEM)
    return pl.pallas_call(
        functools.partial(up_kernel, slots),
        out_shape=(
            jax.ShapeDtypeStruct((parts, ROUTED // parts + 16, w_up.shape[1]), BF),
            jax.ShapeDtypeStruct((16, rows.shape[0] // 2), I32),
        ),
        in_specs=[pl.BlockSpec(memory_space=pltpu.SMEM)] * 2 + [vmem] * 4,
        out_specs=(vmem, vmem),
        compiler_params=pltpu.CompilerParams(vmem_limit_bytes=40 * 1024 * 1024),
    )(core.reshape(1), seq_rank.reshape(1), rows, gain, route, w_up)


def gelu_kernel(packed_ref, out_ref):
    parts, height, hidden_width = packed_ref.shape
    chunk = height - 16
    summed = packed_ref[0].astype(F32)
    for m in range(1, parts):
        summed += packed_ref[m].astype(F32)
    sums = jnp.transpose(summed[chunk:, :chunk])
    inverse = lax.rsqrt((sums[:, :1] + sums[:, 1:2]) / D + 1e-06)
    scores = jax.nn.sigmoid((sums[:, 2:3] + sums[:, 3:4]) * inverse)
    hidden = jax.nn.gelu(summed[:chunk] * inverse, approximate=True) * scores
    hidden = hidden.astype(BF)
    half = chunk // 2
    for side in range(2):
        for m in range(parts):
            out_ref[side * parts + m] = hidden[side * half : (side + 1) * half]


def gelu_call(packed):
    parts, height, hidden_width = packed.shape
    vmem = pl.BlockSpec(memory_space=pltpu.VMEM)
    return pl.pallas_call(
        gelu_kernel,
        out_shape=jax.ShapeDtypeStruct((2 * parts, (height - 16) // 2, hidden_width), BF),
        in_specs=[vmem],
        out_specs=vmem,
        compiler_params=pltpu.CompilerParams(vmem_limit_bytes=32 * 1024 * 1024),
    )(packed)


def per_device(tokens, heavy_index, norm_gain, router, w_up, w_down):
    tok_rows, width = tokens.shape
    slots = heavy_index.shape[0]
    hidden_width = w_up.shape[1]
    chips = lax.axis_size("y")
    parts = lax.axis_size("mp")
    core = lax.axis_index("core")
    used_rows = ROUTED
    share = slots // 2
    seq_rank = lax.axis_index("y") * 2 + core
    local_index = heavy_index - seq_rank * tok_rows
    token_iota = jnp.arange(tok_rows, dtype=I32)
    picker = (local_index[:, None] == token_iota[None, :]).astype(BF)
    selected = jnp.dot(picker, tokens, preferred_element_type=F32)
    selected = jnp.where(local_index[:, None] >= 0, selected, EMPTY)

    rows = lax.all_gather((selected * SCALE).astype(F16), ("y", "core"), tiled=True)
    rows = (rows.astype(F32) * (1.0 / SCALE)).astype(BF)
    gain = norm_gain[None]
    route = gain * router.astype(F32)[None]
    packed, place = up_call(core, seq_rank, rows, gain, route, w_up, slots, parts)
    packed = lax.all_to_all(packed, "mp", 0, 0, tiled=True)
    packed, place, local_index = lax.optimization_barrier((packed, place, local_index))
    mine, start = place[0], place[8]
    pairs = local_index.reshape(share, 2).T
    evens = jnp.broadcast_to(pairs[None], (chips, 2, share)).reshape(chips * slots)
    odds = jnp.broadcast_to(pairs[None, ::-1], (chips, 2, share)).reshape(chips * slots)
    targets = jnp.where(start % 2 == 0, evens, odds)
    hidden = lax.all_to_all(
        gelu_call(packed), ("core", "mp"), 0, 0, tiled=True
    ).reshape(2, used_rows // 2, hidden_width)
    hidden, targets = lax.optimization_barrier((hidden, targets))
    w_near = lax.ppermute(w_down, "core", [(0, 1), (1, 0)])
    here = jnp.where(core == 0, hidden[0], hidden[1])
    near = jnp.where(core == 0, hidden[1], hidden[0])

    expander = (mine[:, None] == jnp.arange(used_rows // 2, dtype=I32)[None, :]).astype(BF)
    wanted = jnp.dot(
        expander, jnp.concatenate([here, near], axis=1), preferred_element_type=F32
    ).astype(BF)
    wanted = lax.optimization_barrier(wanted)
    down = jnp.dot(wanted[:, :hidden_width], w_down, preferred_element_type=F32)
    down += jnp.dot(wanted[:, hidden_width:], w_near, preferred_element_type=F32)
    chip_sum = down.astype(BF).reshape(2 * chips, share, width)
    terms = lax.all_to_all(chip_sum, ("y", "core"), 0, 0, tiled=True).reshape(-1, width)
    placer = (targets[:, None] == token_iota[None, :]).astype(BF)
    placed = lax.dot_general(
        placer, terms, (((0,), (0,)), ((), ())), preferred_element_type=F32
    )
    return (tokens.astype(F32) + placed).astype(BF)


def solution(mesh):
    dp, seq, mp = mesh.devices.shape
    fine = Mesh(mesh.devices.reshape(dp, seq // 2, 2, mp), ("dp", "y", "core", "mp"))
    seq = ("y", "core")
    rows = ("dp",) + seq
    placed = (P(rows, "mp"), P(rows), P("mp"), P("mp"), P("mp", seq), P(seq, "mp"))
    return jax.shard_map(
        per_device, mesh=fine, in_specs=placed, out_specs=P(rows, "mp"), check_vma=False
    )
```
